32 devices in a mesh: groups: 2 (over y), wide: 4 (over z), narrow: 2 (over x), sub: 2 (over core).
Axes of the slice: x: 2, y: 2, z: 4, core: 2. Of those that a mesh axis runs over, the one named last changes fastest.
Arguments:
- tokens: bfloat16 [1024, 13312], P('groups', ('wide', 'narrow', 'sub')), parts along dimension 0, may hold values from -6 to 6
- w_up: bfloat16 [13312, 29696], P('wide', ('narrow', 'sub')), may hold values from -0.078125 to 0.078125
- w_down: bfloat16 [29696, 13312], P(('narrow', 'sub'), 'wide'), may hold values from -0.046875 to 0.046875
Outputs:
- block_out: bfloat16 [1024, 13312], P('groups', ('wide', 'narrow', 'sub')), parts along dimension 0
The draws below stay inside these ranges and needn't reach their ends.
There are 2 independent parts, one for each index of `groups`. The reference program is written for one: setup_inputs(seed, part) draws one part's arguments, and reference() takes and returns one part's arrays. A program takes and returns all parts, laid end to end along the dimension named above; an argument that names none is the same for every part. Nothing has to cross between parts.
All inputs are finite; a program needn't handle non-finite values.
Results may differ from the reference program's by a relative error of at most 0.039.
Values may be sent and summed in bfloat16 or wider, within the bound.
No kernel may reach another device: no remote copies, remote signals or barrier semaphores. Data moves between devices by JAX's collectives and lax.ppermute only.
A program may use at most 192 MiB of HBM per device.

```python
import jax
import jax.numpy as jnp
from jax import lax

D = 13312
FF = 29696
TOK = 512
DBLK = 3328
HBLK = 7424


def strengthened(array, own_key, source, target, shards_of, factor):
    def block_of(axis_at):
        return (jnp.arange(array.shape[axis_at]) // (array.shape[axis_at] // shards_of)).reshape((-1,) + (1,) * (array.ndim - 1 - axis_at))

    first = jax.random.permutation(own_key, shards_of)[block_of(target)]
    second = (block_of(target) + shards_of // 2) % shards_of
    return jnp.where((block_of(source) == first) | (block_of(source) == second), factor * array, array)


def shard_levels(rng, dims, split, smallest, largest):
    def one(axis_at, blocks):
        draws = jax.random.uniform(jax.random.fold_in(jax.random.fold_in(rng, 6), axis_at), (blocks,), jnp.float32, smallest / len(split), largest / len(split))
        return jnp.repeat(jnp.exp(draws), dims[axis_at] // blocks).reshape((-1,) + (1,) * (len(dims) - axis_at - 1))

    level = one(*split[0])
    for cut in split[1:]:
        level = level * one(*cut)
    return level


def scatter_about(stream_key, dims, scale, limit, cuts=(), held_as=jnp.bfloat16):
    loudness = shard_levels(stream_key, dims, cuts, -0.22, 0.18) if cuts else 1.0
    entries = jax.random.normal(stream_key, dims, jnp.float32) * scale * loudness
    return jnp.minimum(jnp.maximum(entries, -limit), limit).astype(held_as)


def bell_draw_with(stream_key, dims, scale, most, shards, heavy, kind=jnp.bfloat16):
    array = scale * jax.random.normal(stream_key, dims, jnp.float32)
    if shards:
        array = array * shard_levels(stream_key, dims, shards, -0.22, 0.18)
    return jnp.clip(strengthened(array, jax.random.fold_in(stream_key, 3), *heavy), -most, most).astype(kind)


def setup_inputs(seed: int = 0, part: int = 0) -> dict:
    key_of = jax.random.split(jax.random.key(seed), 4)
    part_splits = jax.random.split(jax.random.fold_in(key_of[3], part), 4)
    tokens = scatter_about(part_splits[0], (TOK, D), 1.0, 6.0, ((1, 16),))
    w_up = bell_draw_with(key_of[1], (D, FF), D ** -0.5, 0.078125, ((0, 4), (1, 4)), (0, 1, 4, 2.0))
    w_down = bell_draw_with(key_of[2], (FF, D), FF ** -0.5, 0.046875, ((0, 4), (1, 4)), (0, 1, 4, 2.0))
    return {"tokens": tokens, "w_up": w_up, "w_down": w_down}


def blocked_product(left, right, count, width):
    def add_block(index, total):
        start = (index * width).astype(jnp.int32)
        piece_left = lax.dynamic_slice_in_dim(left, start, width, 1)
        piece_right = lax.dynamic_slice_in_dim(right, start, width, 0)
        term = jnp.dot(piece_left, piece_right, preferred_element_type=jnp.float32).astype(jnp.bfloat16)
        term = lax.optimization_barrier(term)
        return total + term.astype(jnp.float32)

    start_total = jnp.zeros((left.shape[0], right.shape[1]), jnp.float32)
    return lax.fori_loop(0, count, add_block, start_total)


def reference(tokens, w_up, w_down):
    pre = blocked_product(tokens, w_up, D // DBLK, DBLK)
    hidden = jax.nn.gelu(pre, approximate=False).astype(jnp.bfloat16)
    summed = blocked_product(hidden, w_down, FF // HBLK, HBLK)
    return summed.astype(jnp.bfloat16)
```

```python
import jax
import jax.numpy as jnp
from jax import lax
from jax.experimental import pallas as pl
from jax.experimental.pallas import tpu as pltpu
from jax.sharding import PartitionSpec as P

F32, BF16 = jnp.float32, jnp.bfloat16
BLOCK = 256
IN_FLIGHT = 3
VMEM_LIMIT = 30 * 2**20
LONG = pl.CostEstimate(flops=10**12, bytes_accessed=10**9, transcendentals=0)
SHORT = pl.CostEstimate(flops=10**3, bytes_accessed=10**3, transcendentals=0)
SWAP = [(0, 1), (1, 0)]


def gelu(v):
    return 0.5 * v * (1.0 + lax.erf(v * (0.5**0.5)))


def tiles_of(row, rows, column, widths):
    out = []
    for width in widths:
        out.append((row, rows, column, width))
        column += width
    return out


def plan(rows, columns):
    half = rows // 2
    head, tail = [1024, 1024], [512, 256]
    middle = columns - sum(head) - sum(tail)
    even = [1024] * (middle // 1024) + ([middle % 1024] if middle % 1024 else [])
    return (
        tiles_of(0, half, 0, head)
        + tiles_of(half, half, 0, head)
        + tiles_of(0, rows, sum(head), even)
        + tiles_of(0, rows, columns - sum(tail), tail)
    )


class Chain:
    def __init__(self, token):
        self.token = token

    def call(self, body, ins, outs, scratch=(), alias=None, name=None, gates=(), cost=SHORT):
        spaces = [space for _, space in ins]
        arrays = [pltpu.with_memory_space_constraint(a, pltpu.VMEM) if s == pltpu.VMEM else a for a, s in ins]
        n_in, n_out = len(ins), len(outs)
        extra = [self.token, *gates]

        def kernel(*refs):
            at = n_in + len(extra)
            body(refs[:n_in], refs[at : at + n_out], refs[at + n_out + len(extra) :])

        aliases = dict(alias or {})
        for i in range(len(extra)):
            aliases[n_in + i] = n_out + i
        anywhere = [pl.BlockSpec(memory_space=pl.ANY)] * len(extra)
        got = pl.pallas_call(
            kernel,
            in_specs=[pl.BlockSpec(memory_space=s) for s in spaces] + anywhere,
            out_specs=[pl.BlockSpec(memory_space=pltpu.VMEM)] * n_out + anywhere,
            out_shape=[pltpu.VMEM(shape, dtype) for shape, dtype in outs]
            + [jax.ShapeDtypeStruct(e.shape, e.dtype) for e in extra],
            scratch_shapes=list(scratch),
            input_output_aliases=aliases,
            compiler_params=pltpu.CompilerParams(vmem_limit_bytes=VMEM_LIMIT),
            cost_estimate=cost,
            name=name,
        )(*arrays, *extra)
        self.token = got[n_out]
        return list(got[:n_out]), list(got[n_out + 1 :])


def by_rows(rows, step, work):
    @pl.loop(0, rows // step)
    def _(i):
        work(pl.ds(pl.multiple_of(i * step, step), step))


def step_kernel(chain, up, add, act, down, at_end, name, gates=()):
    ins, outs, scratch, alias, where = [], [], [], {}, {}
    blocks_up = up[2][3] // BLOCK if up else 0
    blocks_down = down[3][3] // BLOCK if down else 0
    if add:
        where["add"] = (len(ins), len(outs))
        ins += [(add[0], pltpu.VMEM), (add[1], pltpu.VMEM)]
        outs.append((add[0].shape, BF16))
    if act:
        where["act"] = (len(ins), len(outs))
        ins += [(act[0], pltpu.VMEM), (act[1], pltpu.VMEM)]
        outs.append((act[0].shape, BF16))
    if up:
        xs, w_up, (_, rows_up, column_up, _) = up
        where["up"] = (len(ins), len(outs), len(scratch))
        ins += [(w_up, pl.ANY)] + [(x, pltpu.VMEM) for x in xs]
        outs.append(((rows_up, up[2][3]), BF16))
        scratch += [pltpu.VMEM((blocks_up, w_up.shape[0], BLOCK), BF16), pltpu.SemaphoreType.DMA((blocks_up,))]
    if down:
        mine, sent, w_down, (row, rows, column, _), total, shape, first = down
        where["down"] = (len(ins), len(outs), len(scratch))
        ins += [(mine, pltpu.VMEM), (sent, pltpu.VMEM), (at_end, pltpu.SMEM), (w_down, pl.ANY)]
        if total is not None:
            alias[len(ins)] = len(outs)
            ins.append((total, pltpu.VMEM))
        outs.append((shape, F32))
        scratch += [
            pltpu.VMEM((blocks_down, BLOCK, w_down.shape[1]), BF16),
            pltpu.SemaphoreType.DMA((blocks_down,)),
        ]

    def body(in_refs, out_refs, scratch_refs):
        def up_copy(i):
            i0, _, s0 = where["up"]
            columns = pl.ds(pl.multiple_of(column_up + i * BLOCK, BLOCK), BLOCK)
            return pltpu.make_async_copy(
                in_refs[i0].at[:, columns], scratch_refs[s0].at[i], scratch_refs[s0 + 1].at[i]
            )

        def down_copy(i):
            i0, _, s0 = where["down"]
            return pltpu.make_async_copy(
                in_refs[i0 + 3].at[pl.ds(column + i * BLOCK, BLOCK), :],
                scratch_refs[s0].at[i],
                scratch_refs[s0 + 1].at[i],
            )

        for i in range(min(IN_FLIGHT, blocks_up)):
            up_copy(i).start()
        ahead = min(IN_FLIGHT - min(IN_FLIGHT, blocks_up), blocks_down)
        for i in range(ahead):
            down_copy(i).start()

        if add:
            i0, o0 = where["add"]

            def sum_rows(r):
                out_refs[o0][r, :] = (in_refs[i0][r, :].astype(F32) + in_refs[i0 + 1][r, :].astype(F32)).astype(BF16)

            by_rows(add[0].shape[0], 16, sum_rows)
        if act:
            i1, o1 = where["act"]

            def activate(r):
                v = in_refs[i1][r, :].astype(F32) + in_refs[i1 + 1][r, :].astype(F32)
                out_refs[o1][r, :] = gelu(v).astype(BF16)

            by_rows(act[0].shape[0], 16, activate)
        if up:
            i0, o0, s0 = where["up"]

            @pl.loop(0, blocks_up)
            def _(i):
                up_copy(i).wait()

                @pl.when(i + IN_FLIGHT < blocks_up)
                def _():
                    up_copy(i + IN_FLIGHT).start()

                columns = pl.ds(pl.multiple_of(i * BLOCK, BLOCK), BLOCK)
                at = 0
                for k, x in enumerate(xs):
                    out_refs[o0][at : at + x.shape[0], columns] = jnp.dot(
                        in_refs[i0 + 1 + k][...], scratch_refs[s0][i], preferred_element_type=F32
                    ).astype(BF16)
                    at += x.shape[0]

        if down:
            i0, o0, s0 = where["down"]
            takes = in_refs[i0 + 2][0] > 0
            for i in range(ahead, min(IN_FLIGHT, blocks_down)):
                down_copy(i).start()
            for i in range(blocks_down):
                down_copy(i).wait()
                if i + IN_FLIGHT < blocks_down:
                    down_copy(i + IN_FLIGHT).start()
                units = slice(i * BLOCK, (i + 1) * BLOCK)
                h = jnp.where(takes, in_refs[i0 + 1][:, units], in_refs[i0][:, units])
                term = jnp.dot(h, scratch_refs[s0][i], preferred_element_type=F32)
                if first and i == 0:
                    out_refs[o0][row : row + rows, :] = term
                else:
                    out_refs[o0][row : row + rows, :] += term

    got, passed = chain.call(body, ins, outs, scratch, alias, name, gates, LONG)
    result = {key: got[at[1]] for key, at in where.items()}
    return result, passed


def split_rows(chain, features, cut):
    f, rows = features.shape

    def body(in_refs, out_refs, _):
        out_refs[0][...] = in_refs[0][:, :cut]
        out_refs[1][...] = in_refs[0][:, cut:]

    got, _ = chain.call(body, [(features, pltpu.VMEM)], [((f, cut), BF16), ((f, rows - cut), BF16)], name="split_rows")
    return got


def place_features(chain, place, pieces, name, gates=()):
    f, rows = pieces[0].shape

    def body(in_refs, out_refs, scratch):
        held = scratch[0]
        for mine in range(4):

            @pl.when(in_refs[4][0] == mine)
            def _(mine=mine):
                for q in range(4):
                    held[q * f : (q + 1) * f, :] = in_refs[mine ^ q][...]

        for c in range(0, rows, 128):
            out_refs[0][c : c + 128, :] = held[:, c : c + 128].T

    ins = [(p, pltpu.VMEM) for p in pieces] + [(place, pltpu.SMEM)]
    (x,), passed = chain.call(
        body, ins, [((rows, 4 * f), BF16)], [pltpu.VMEM((4 * f, rows), BF16)], None, name, gates
    )
    return x, passed


def part_features(chain, place, total, row, rows, name, gates=()):
    features = total.shape[1]
    f = features // 4

    def body(in_refs, out_refs, scratch):
        held = scratch[0]
        for c in range(rows // 128):
            held[:, c * 128 : (c + 1) * 128] = (
                in_refs[0][row + c * 128 : row + (c + 1) * 128, :].astype(BF16).T
            )
        for mine in range(4):

            @pl.when(in_refs[1][0] == mine)
            def _(mine=mine):
                for out, slot, q in ((0, 0, mine), (0, 1, mine ^ 2), (1, 0, mine ^ 1), (1, 1, mine ^ 3)):
                    out_refs[out][slot] = held[q * f : (q + 1) * f, :]

    both = ((2, f, rows), BF16)
    (keep, give), passed = chain.call(
        body, [(total, pltpu.VMEM), (place, pltpu.SMEM)], [both, both], [pltpu.VMEM((features, rows), BF16)], None, name, gates
    )
    return keep, give


def add_chip(chain, keep, got, name):
    shape = keep.shape[1:]

    def body(in_refs, out_refs, _):
        for slot in range(2):

            def sum_rows(r, slot=slot):
                out_refs[slot][r, :] = (
                    in_refs[0][slot, r, :].astype(F32) + in_refs[1][slot, r, :].astype(F32)
                ).astype(out_refs[slot].dtype)

            by_rows(shape[0], 16, sum_rows)

    (near, far), _ = chain.call(
        body, [(keep, pltpu.VMEM), (got, pltpu.VMEM)], [(shape, F32), (shape, BF16)], name=name
    )
    return near, far


def finish(chain, near, across, out, shape, row, name):
    f, rows = near.shape
    ins, alias = [(near, pltpu.VMEM), (across, pltpu.VMEM)], {}
    if out is not None:
        alias[len(ins)] = 0
        ins.append((out, pltpu.VMEM))

    def body(in_refs, out_refs, _):
        def sum_rows(r):
            out_refs[0][r, row : row + rows] = (in_refs[0][r, :] + in_refs[1][r, :].astype(F32)).astype(BF16)

        by_rows(f, 16, sum_rows)

    (got,), _ = chain.call(body, ins, [(shape, BF16)], alias=alias, name=name)
    return got


def pipelined(tokens, w_up, w_down):
    rows = tokens.shape[0]
    features = tokens.T
    half = rows // 2
    at = lax.axis_index("wide")
    at_end = ((at == 0) | (at == 3)).astype(jnp.int32).reshape(1)
    place = (lax.axis_index("narrow") * 2 + lax.axis_index("sub")).astype(jnp.int32).reshape(1)
    inward, middle, outward = [(0, 1), (3, 2)], [(1, 2), (2, 1)], [(1, 0), (2, 3)]

    chain = Chain(jnp.zeros((8, 128), F32))
    sum_shape = (rows, w_down.shape[1])
    tiles = plan(rows, w_up.shape[1])
    n = len(tiles)

    low, high = split_rows(chain, features, half)
    across = lax.ppermute(low, "narrow", SWAP)
    sibling, corner = lax.ppermute(low, "sub", SWAP), lax.ppermute(across, "sub", SWAP)
    x_low, (high,) = place_features(chain, place, [low, sibling, across, corner], "place_low", gates=(high,))
    xs = {0: x_low}
    across = lax.ppermute(high, "narrow", SWAP)
    sibling = lax.ppermute(high, "sub", SWAP)

    part, summed, hidden = {}, {}, {}
    met_in, met_mid, met_out = {}, {}, {}
    total, seen = None, []
    for t in range(n + 6):
        a, g, d = t - 2, t - 4, t - 6
        up = add = act = down = None
        gates = ()
        if t < n:
            if t == 1:
                gates = (across, sibling)
            if t == 2:
                xs[half], _ = place_features(chain, place, [high, sibling, across, corner], "place_high")
            up = ([xs[r] for r in (0, half) if tiles[t][0] <= r < tiles[t][0] + tiles[t][1]], w_up, tiles[t])
        if 0 <= a < n:
            add = (part[a], met_in[a])
        if 0 <= g < n:
            act = (summed[g], met_mid[g])
        if 0 <= d < n:
            first = not any(r < tiles[d][0] + tiles[d][1] and tiles[d][0] < r + k for r, k in seen)
            seen.append(tiles[d][:2])
            down = (hidden[d], met_out[d], w_down, tiles[d], total, sum_shape, first)
        got, passed = step_kernel(chain, up, add, act, down, at_end, f"step_{t}", gates)
        if passed:
            across, sibling = passed
            corner = lax.ppermute(across, "sub", SWAP)
        if up:
            part[t] = got["up"]
            met_in[t] = lax.ppermute(got["up"], "wide", inward)
        if add:
            summed[a] = got["add"]
            met_mid[a] = lax.ppermute(got["add"], "wide", middle)
        if act:
            hidden[g] = got["act"]
            met_out[g] = lax.ppermute(got["act"], "wide", outward)
        if down:
            total = got["down"]

    out_shape = features.shape
    halves = []
    for i, row in enumerate((0, half)):
        keep, give = part_features(chain, place, total, row, half, f"part_{i}")
        halves.append((keep, lax.ppermute(give, "sub", SWAP)))
    far = []
    for i, (keep, got) in enumerate(halves):
        near, chip = add_chip(chain, keep, got, f"add_chip_{i}")
        far.append((near, lax.ppermute(chip, "narrow", SWAP)))
    out = None
    for i, (near, across) in enumerate(far):
        out = finish(chain, near, across, out, out_shape, i * half, f"finish_{i}")
    return out.T


def collective(tokens, w_up, w_down):
    gathered = lax.all_gather(tokens, ("narrow", "sub"), axis=1, tiled=True)
    block_up = jnp.dot(gathered, w_up, preferred_element_type=F32).astype(BF16)
    pre = lax.psum_scatter(block_up, "wide", scatter_dimension=1, tiled=True).astype(F32)
    hidden = lax.all_gather(gelu(pre).astype(BF16), "wide", axis=1, tiled=True)
    block_down = jnp.dot(hidden, w_down, preferred_element_type=F32).astype(BF16)
    return lax.psum_scatter(block_down, ("narrow", "sub"), scatter_dimension=1, tiled=True)


def solution(mesh):
    placed = (
        P("groups", ("wide", "narrow", "sub")),
        P("wide", ("narrow", "sub")),
        P(("narrow", "sub"), "wide"),
    )
    small = (mesh.shape["wide"], mesh.shape["narrow"], mesh.shape["sub"]) == (4, 2, 2)
    return jax.shard_map(
        pipelined if small else collective,
        mesh=mesh,
        in_specs=placed,
        out_specs=P("groups", ("wide", "narrow", "sub")),
        check_vma=False,
    )
```

```python
import jax
import jax.numpy as jnp
from jax import lax
from jax.experimental import pallas as pl
from jax.experimental.pallas import tpu as pltpu
from jax.sharding import PartitionSpec as P

F32, BF16 = jnp.float32, jnp.bfloat16
BLOCK = 256
IN_FLIGHT = 3
VMEM_LIMIT = 30 * 2**20
STEP_COST = 10 * 10**9
SHORT = pl.CostEstimate(flops=10**3, bytes_accessed=10**3, transcendentals=0)
SWAP = [(0, 1), (1, 0)]


def gelu(v):
    return 0.5 * v * (1.0 + lax.erf(v * (0.5**0.5)))


def tiles_of(row, rows, column, widths):
    out = []
    for width in widths:
        out.append((row, rows, column, width))
        column += width
    return out


def estimate(flops):
    return pl.CostEstimate(flops=flops, bytes_accessed=0, transcendentals=0)


def plan(rows, columns):
    half = rows // 2
    head, tail, last = [1024, 1024], [1024, 768], [1024, 768]
    middle = columns - sum(head) - sum(tail)
    wide = 512
    even = [wide] * (middle // wide) + ([middle % wide] if middle % wide else [])
    return (
        tiles_of(0, half, 0, head)
        + tiles_of(half, half, 0, head)
        + tiles_of(0, rows, sum(head), even)
        + tiles_of(half, half, columns - sum(tail), tail)
        + tiles_of(0, half, columns - sum(tail), last)
    )


def folded(tile, whole):
    blocks, folds = tile[3] // BLOCK, whole // tile[1]
    across = blocks // folds if blocks % folds == 0 else 1
    return blocks // across * tile[1], across * BLOCK


class Chain:
    def __init__(self, token):
        self.token = token

    def call(self, body, ins, outs, scratch=(), alias=None, name=None, gates=(), cost=SHORT):
        spaces = [space for _, space in ins]
        arrays = [pltpu.with_memory_space_constraint(a, pltpu.VMEM) if s == pltpu.VMEM else a for a, s in ins]
        n_in, n_out = len(ins), len(outs)
        extra = [self.token, *gates]

        def kernel(*refs):
            at = n_in + len(extra)
            body(refs[:n_in], refs[at : at + n_out], refs[at + n_out + len(extra) :])

        aliases = dict(alias or {})
        for i in range(len(extra)):
            aliases[n_in + i] = n_out + i
        anywhere = [pl.BlockSpec(memory_space=pl.ANY)] * len(extra)
        got = pl.pallas_call(
            kernel,
            in_specs=[pl.BlockSpec(memory_space=s) for s in spaces] + anywhere,
            out_specs=[pl.BlockSpec(memory_space=pltpu.VMEM)] * n_out + anywhere,
            out_shape=[pltpu.VMEM(shape, dtype) for shape, dtype in outs]
            + [jax.ShapeDtypeStruct(e.shape, e.dtype) for e in extra],
            scratch_shapes=list(scratch),
            input_output_aliases=aliases,
            compiler_params=pltpu.CompilerParams(vmem_limit_bytes=VMEM_LIMIT),
            cost_estimate=cost,
            name=name,
        )(*arrays, *extra)
        self.token = got[n_out]
        return list(got[:n_out]), list(got[n_out + 1 :])


def by_rows(rows, step, work):
    @pl.loop(0, rows // step)
    def _(i):
        work(pl.ds(pl.multiple_of(i * step, step), step))


def step_kernel(chain, at_end, name, cost, whole, up=None, add=None, act=None, down=None, gates=()):
    ins, outs, scratch, alias, where = [(at_end, pltpu.SMEM)], [], [], {}, {}
    blocks_up = up[2][3] // BLOCK if up else 0
    blocks_down = down[3][3] // BLOCK if down else 0
    merged = bool(up and act) and folded(up[2], whole) == act[0].shape
    if add:
        where["add"] = (len(ins), len(outs))
        ins += [(add[0], pltpu.VMEM), (add[1], pltpu.VMEM)]
        outs.append((add[0].shape, BF16))
    if act:
        where["act"] = (len(ins), len(outs))
        ins += [(act[0], pltpu.VMEM), (act[1], pltpu.VMEM)]
        outs.append((act[0].shape, BF16))
    if up:
        xs, w_up, (_, rows_up, column_up, _) = up
        where["up"] = (len(ins), len(outs), len(scratch))
        ins += [(w_up, pl.ANY)] + [(x, pltpu.VMEM) for x in xs]
        shape_up = folded(up[2], whole)
        outs.append((shape_up, BF16))
        scratch += [pltpu.VMEM((blocks_up, w_up.shape[0], BLOCK), BF16), pltpu.SemaphoreType.DMA((blocks_up,))]
    if down:
        mine, sent, w_down, (row, rows, column, _), total, shape, first = down
        where["down"] = (len(ins), len(outs), len(scratch))
        ins += [(mine, pltpu.VMEM), (sent, pltpu.VMEM), (w_down, pl.ANY)]
        if total is not None:
            alias[len(ins)] = len(outs)
            ins.append((total, pltpu.VMEM))
        outs.append((shape, F32))
        scratch += [
            pltpu.VMEM((blocks_down, BLOCK, w_down.shape[1]), BF16),
            pltpu.SemaphoreType.DMA((blocks_down,)),
        ]

    def body(in_refs, out_refs, scratch_refs):
        end = in_refs[0][0] > 0

        def up_copy(i):
            i0, _, s0 = where["up"]
            columns = pl.ds(pl.multiple_of(column_up + i * BLOCK, BLOCK), BLOCK)
            return pltpu.make_async_copy(
                in_refs[i0].at[:, columns], scratch_refs[s0].at[i], scratch_refs[s0 + 1].at[i]
            )

        def down_copy(i):
            i0, _, s0 = where["down"]
            return pltpu.make_async_copy(
                in_refs[i0 + 2].at[pl.ds(column + i * BLOCK, BLOCK), :],
                scratch_refs[s0].at[i],
                scratch_refs[s0 + 1].at[i],
            )

        for i in range(min(IN_FLIGHT, blocks_up)):
            up_copy(i).start()
        for i in range(min(IN_FLIGHT, blocks_down)):
            down_copy(i).start()

        if add:
            i0, o0 = where["add"]

            def sum_rows(r):
                out_refs[o0][r, :] = (in_refs[i0][r, :].astype(F32) + in_refs[i0 + 1][r, :].astype(F32)).astype(BF16)

            by_rows(add[0].shape[0], 16, sum_rows)
        if act:
            i1, o1 = where["act"]

            @pl.when(jnp.logical_not(end))
            def _():
                def activate(r):
                    v = in_refs[i1][r, :].astype(F32) + in_refs[i1 + 1][r, :].astype(F32)
                    out_refs[o1][r, :] = gelu(v).astype(BF16)

                by_rows(act[0].shape[0], 16, activate)

        if up:
            i2, o2, s2 = where["up"]

            @pl.loop(0, blocks_up)
            def _(i):
                up_copy(i).wait()

                @pl.when(i + IN_FLIGHT < blocks_up)
                def _():
                    up_copy(i + IN_FLIGHT).start()

                across = shape_up[1] // BLOCK
                columns = pl.ds(pl.multiple_of(i % across * BLOCK, BLOCK), BLOCK)
                begin = pl.multiple_of(i // across * rows_up, rows_up)
                at = 0
                for k, x in enumerate(xs):
                    span = pl.ds(begin + at, x.shape[0])
                    out_refs[o2][span, columns] = jnp.dot(
                        in_refs[i2 + 1 + k][...], scratch_refs[s2][i], preferred_element_type=F32
                    ).astype(BF16)
                    at += x.shape[0]

                if merged:

                    @pl.when(end)
                    def _():
                        span = pl.ds(begin, rows_up)
                        out_refs[where["act"][1]][span, columns] = out_refs[o2][span, columns]

        if down:
            i3, o3, s3 = where["down"]
            for i in range(blocks_down):
                down_copy(i).wait()
                if i + IN_FLIGHT < blocks_down:
                    down_copy(i + IN_FLIGHT).start()
                across = mine.shape[1] // BLOCK
                units = slice(i % across * BLOCK, (i % across + 1) * BLOCK)
                span = slice(i // across * rows, (i // across + 1) * rows)
                h = jnp.where(end, in_refs[i3 + 1][span, units], in_refs[i3][span, units])
                term = jnp.dot(h, scratch_refs[s3][i], preferred_element_type=F32)
                if first and i == 0:
                    out_refs[o3][row : row + rows, :] = term
                else:
                    out_refs[o3][row : row + rows, :] += term

    got, passed = chain.call(body, ins, outs, scratch, alias, name, gates, cost)
    return {key: got[at[1]] for key, at in where.items()}, passed, merged


def split_rows(chain, features, cut):
    f, rows = features.shape

    def body(in_refs, out_refs, _):
        out_refs[0][...] = in_refs[0][:, :cut]
        out_refs[1][...] = in_refs[0][:, cut:]

    got, _ = chain.call(body, [(features, pltpu.VMEM)], [((f, cut), BF16), ((f, rows - cut), BF16)], name="split_rows")
    return got


def place_features(chain, place, pieces, name, gates=()):
    f, rows = pieces[0].shape

    def body(in_refs, out_refs, scratch):
        held = scratch[0]
        for mine in range(4):

            @pl.when(in_refs[4][0] == mine)
            def _(mine=mine):
                for q in range(4):
                    held[q * f : (q + 1) * f, :] = in_refs[mine ^ q][...]

        for c in range(0, rows, 128):
            out_refs[0][c : c + 128, :] = held[:, c : c + 128].T

    ins = [(p, pltpu.VMEM) for p in pieces] + [(place, pltpu.SMEM)]
    (x,), passed = chain.call(
        body, ins, [((rows, 4 * f), BF16)], [pltpu.VMEM((4 * f, rows), BF16)], None, name, gates
    )
    return x, passed


def part_features(chain, place, total, row, rows, name, gates=()):
    features = total.shape[1]
    f = features // 4

    def body(in_refs, out_refs, scratch):
        held = scratch[0]
        for c in range(rows // 128):
            held[:, c * 128 : (c + 1) * 128] = (
                in_refs[0][row + c * 128 : row + (c + 1) * 128, :].astype(BF16).T
            )
        for mine in range(4):

            @pl.when(in_refs[1][0] == mine)
            def _(mine=mine):
                for out, slot, q in ((0, 0, mine), (0, 1, mine ^ 2), (1, 0, mine ^ 1), (1, 1, mine ^ 3)):
                    out_refs[out][slot] = held[q * f : (q + 1) * f, :]

    both = ((2, f, rows), BF16)
    (keep, give), passed = chain.call(
        body, [(total, pltpu.VMEM), (place, pltpu.SMEM)], [both, both], [pltpu.VMEM((features, rows), BF16)], None, name, gates
    )
    return keep, give


def add_chip(chain, keep, got, name):
    shape = keep.shape[1:]

    def body(in_refs, out_refs, _):
        for slot in range(2):

            def sum_rows(r, slot=slot):
                out_refs[slot][r, :] = (
                    in_refs[0][slot, r, :].astype(F32) + in_refs[1][slot, r, :].astype(F32)
                ).astype(out_refs[slot].dtype)

            by_rows(shape[0], 16, sum_rows)

    (near, far), _ = chain.call(
        body, [(keep, pltpu.VMEM), (got, pltpu.VMEM)], [(shape, F32), (shape, BF16)], name=name
    )
    return near, far


def finish(chain, near, across, out, shape, row, name):
    f, rows = near.shape
    ins, alias = [(near, pltpu.VMEM), (across, pltpu.VMEM)], {}
    if out is not None:
        alias[len(ins)] = 0
        ins.append((out, pltpu.VMEM))

    def body(in_refs, out_refs, _):
        def sum_rows(r):
            out_refs[0][r, row : row + rows] = (in_refs[0][r, :] + in_refs[1][r, :].astype(F32)).astype(BF16)

        by_rows(f, 16, sum_rows)

    (got,), _ = chain.call(body, ins, [(shape, BF16)], alias=alias, name=name)
    return got


def pipelined(tokens, w_up, w_down):
    rows = tokens.shape[0]
    features = tokens.T
    half = rows // 2
    at = lax.axis_index("wide")
    at_end = ((at == 0) | (at == 3)).astype(jnp.int32).reshape(1)
    place = (lax.axis_index("narrow") * 2 + lax.axis_index("sub")).astype(jnp.int32).reshape(1)
    inward, middle, outward = [(0, 1), (3, 2)], [(1, 2), (2, 1)], [(1, 0), (2, 3)]

    chain = Chain(jnp.zeros((8, 128), F32))
    sum_shape = (rows, w_down.shape[1])
    tiles = plan(rows, w_up.shape[1])
    n = len(tiles)

    low, high = split_rows(chain, features, half)
    across = lax.ppermute(low, "narrow", SWAP)
    sibling, corner = lax.ppermute(low, "sub", SWAP), lax.ppermute(across, "sub", SWAP)
    x_low, (high,) = place_features(chain, place, [low, sibling, across, corner], "place_low", gates=(high,))
    xs = {0: x_low}
    across = lax.ppermute(high, "narrow", SWAP)
    sibling = lax.ppermute(high, "sub", SWAP)

    part, summed, hidden = {}, {}, {}
    met_in, met_mid, met_out = {}, {}, {}
    total, seen = None, []
    high_last = max(i for i, tile in enumerate(tiles) if tile[0] + tile[1] > half)
    cost = estimate(STEP_COST)
    for t in range(n + 4):
        g = t - 3
        up = act = None
        gates = ()
        if t < n:
            if t == 1:
                gates = (across, sibling)
            if half not in xs and tiles[t][0] + tiles[t][1] > half:
                xs[half], _ = place_features(chain, place, [high, sibling, across, corner], "place_high")
            up = ([xs[r] for r in (0, half) if tiles[t][0] <= r < tiles[t][0] + tiles[t][1]], w_up, tiles[t])
        if 0 <= g < n:
            act = (summed[g], met_mid[g])
        if up or act:
            got, passed, merged = step_kernel(chain, at_end, f"up_act_{t}", cost, rows, up=up, act=act, gates=gates)
            if passed:
                across, sibling = passed
                corner = lax.ppermute(across, "sub", SWAP)
            if up:
                part[t] = got["up"]
            if act:
                hidden[g] = got["act"]
            if merged:
                met_in[t] = met_out[g] = lax.ppermute(got["act"], "wide", inward + outward)
            else:
                if up:
                    met_in[t] = lax.ppermute(got["up"], "wide", inward)
                if act:
                    met_out[g] = lax.ppermute(got["act"], "wide", outward)
        a, d = t - 1, t - 4
        add = down = None
        if 0 <= a < n:
            add = (part[a], met_in[a])
        if 0 <= d < n:
            first = not any(r < tiles[d][0] + tiles[d][1] and tiles[d][0] < r + k for r, k in seen)
            seen.append(tiles[d][:2])
            down = (hidden[d], met_out[d], w_down, tiles[d], total, sum_shape, first)
        if add or down:
            got, _, _ = step_kernel(chain, at_end, f"add_down_{t}", cost, rows, add=add, down=down)
            if add:
                summed[a] = got["add"]
                met_mid[a] = lax.ppermute(got["add"], "wide", middle)
            if down:
                total = got["down"]
        if d == high_last:
            keep, give = part_features(chain, place, total, half, rows - half, "part_high")
            got_high = lax.ppermute(give, "sub", SWAP)
        if d == high_last + 1:
            near, chip = add_chip(chain, keep, got_high, "add_chip_high")
            high_sum = (near, lax.ppermute(chip, "narrow", SWAP))
            cost = SHORT

    out = finish(chain, *high_sum, None, features.shape, half, "finish_high")
    keep, give = part_features(chain, place, total, 0, half, "part_low")
    near, chip = add_chip(chain, keep, lax.ppermute(give, "sub", SWAP), "add_chip_low")
    across = lax.ppermute(chip, "narrow", SWAP)
    return finish(chain, near, across, out, features.shape, 0, "finish_low").T


def collective(tokens, w_up, w_down):
    gathered = lax.all_gather(tokens, ("narrow", "sub"), axis=1, tiled=True)
    block_up = jnp.dot(gathered, w_up, preferred_element_type=F32).astype(BF16)
    pre = lax.psum_scatter(block_up, "wide", scatter_dimension=1, tiled=True).astype(F32)
    hidden = lax.all_gather(gelu(pre).astype(BF16), "wide", axis=1, tiled=True)
    block_down = jnp.dot(hidden, w_down, preferred_element_type=F32).astype(BF16)
    return lax.psum_scatter(block_down, ("narrow", "sub"), scatter_dimension=1, tiled=True)


def solution(mesh):
    placed = (
        P("groups", ("wide", "narrow", "sub")),
        P("wide", ("narrow", "sub")),
        P(("narrow", "sub"), "wide"),
    )
    small = (mesh.shape["wide"], mesh.shape["narrow"], mesh.shape["sub"]) == (4, 2, 2)
    return jax.shard_map(
        pipelined if small else collective,
        mesh=mesh,
        in_specs=placed,
        out_specs=P("groups", ("wide", "narrow", "sub")),
        check_vma=False,
    )
```

```python
import jax
import jax.numpy as jnp
from jax import lax
from jax.experimental import pallas as pl
from jax.experimental.pallas import tpu as pltpu
from jax.sharding import PartitionSpec as P

F32, BF16 = jnp.float32, jnp.bfloat16
BLOCK = 256
IN_FLIGHT = 3
VMEM_LIMIT = 30 * 2**20
LAG = 3
STEP_COST = 10 * 10**9
SHORT = pl.CostEstimate(flops=10**3, bytes_accessed=10**3, transcendentals=0)
SWAP = [(0, 1), (1, 0)]


def gelu(v):
    return 0.5 * v * (1.0 + lax.erf(v * (0.5**0.5)))


def tiles_of(row, rows, column, widths):
    out = []
    for width in widths:
        out.append((row, rows, column, width))
        column += width
    return out


def estimate(flops):
    return pl.CostEstimate(flops=flops, bytes_accessed=0, transcendentals=0)


def plan(rows, columns):
    half = rows // 2
    head, tail, last = [1024, 1024], [1024, 768], [1024, 768]
    middle = columns - sum(head) - sum(tail)
    wide = 512
    even = [wide] * (middle // wide) + ([middle % wide] if middle % wide else [])
    return (
        tiles_of(0, half, 0, head)
        + tiles_of(half, half, 0, head)
        + tiles_of(0, rows, sum(head), even)
        + tiles_of(half, half, columns - sum(tail), tail)
        + tiles_of(0, half, columns - sum(tail), last)
    )


def folded(tile, whole):
    blocks, folds = tile[3] // BLOCK, whole // tile[1]
    across = blocks // folds if blocks % folds == 0 else 1
    return blocks // across * tile[1], across * BLOCK


class Chain:
    def __init__(self, token):
        self.token = token

    def call(self, body, ins, outs, scratch=(), alias=None, name=None, gates=(), cost=SHORT):
        spaces = [space for _, space in ins]
        arrays = [pltpu.with_memory_space_constraint(a, s) if s in (pltpu.VMEM, pltpu.HBM) else a for a, s in ins]
        n_in, n_out = len(ins), len(outs)
        extra = [self.token, *gates]

        def kernel(*refs):
            at = n_in + len(extra)
            body(refs[:n_in], refs[at : at + n_out], refs[at + n_out + len(extra) :])

        aliases = dict(alias or {})
        for i in range(len(extra)):
            aliases[n_in + i] = n_out + i
        anywhere = [pl.BlockSpec(memory_space=pl.ANY)] * len(extra)
        got = pl.pallas_call(
            kernel,
            in_specs=[pl.BlockSpec(memory_space=s) for s in spaces] + anywhere,
            out_specs=[pl.BlockSpec(memory_space=pltpu.VMEM)] * n_out + anywhere,
            out_shape=[pltpu.VMEM(shape, dtype) for shape, dtype in outs]
            + [jax.ShapeDtypeStruct(e.shape, e.dtype) for e in extra],
            scratch_shapes=list(scratch),
            input_output_aliases=aliases,
            compiler_params=pltpu.CompilerParams(vmem_limit_bytes=VMEM_LIMIT),
            cost_estimate=cost,
            name=name,
        )(*arrays, *extra)
        self.token = got[n_out]
        return list(got[:n_out]), list(got[n_out + 1 :])


def by_rows(rows, step, work):
    @pl.loop(0, rows // step)
    def _(i):
        work(pl.ds(pl.multiple_of(i * step, step), step))


def step_kernel(chain, at_end, name, cost, whole, up=None, add=None, act=None, down=None, gates=(), held=None, ahead=None):
    ins, outs, scratch, alias, where = [(at_end, pltpu.SMEM)], [], [], {}, {}
    blocks_up = up[2][3] // BLOCK if up else 0
    blocks_down = down[3][3] // BLOCK if down else 0
    kept = held.shape[0] if held is not None else 0
    merged = bool(up and act) and folded(up[2], whole) == act[0].shape
    if add:
        where["add"] = (len(ins), len(outs))
        ins += [(add[0], pltpu.VMEM), (add[1], pltpu.VMEM)]
        outs.append((add[0].shape, BF16))
    if act:
        where["act"] = (len(ins), len(outs))
        ins += [(act[0], pltpu.VMEM), (act[1], pltpu.VMEM)]
        outs.append((act[0].shape, BF16))
    if up:
        xs, w_up, (_, rows_up, column_up, _) = up
        where["up"] = (len(ins), len(outs), len(scratch))
        ins += [(w_up, pl.ANY)] + [(x, pltpu.VMEM) for x in xs]
        shape_up = folded(up[2], whole)
        outs.append((shape_up, BF16))
        fresh = max(blocks_up - kept, 1)
        scratch += [pltpu.VMEM((fresh, w_up.shape[0], BLOCK), BF16), pltpu.SemaphoreType.DMA((fresh,))]
    if down:
        mine, sent, w_down, (row, rows, column, _), total, shape, first = down
        where["down"] = (len(ins), len(outs), len(scratch))
        ins += [(mine, pltpu.VMEM), (sent, pltpu.VMEM), (w_down, pl.ANY)]
        if total is not None:
            alias[len(ins)] = len(outs)
            ins.append((total, pltpu.VMEM))
        outs.append((shape, F32))
        fresh = max(blocks_down - kept, 1)
        scratch += [pltpu.VMEM((fresh, BLOCK, w_down.shape[1]), BF16), pltpu.SemaphoreType.DMA((fresh,))]
    if held is not None:
        where["held"] = (len(ins), None)
        ins.append((held, pltpu.VMEM))
    if ahead:
        kind, weights, begin_ahead = ahead
        where["ahead"] = (len(ins), len(outs), len(scratch))
        ins.append((weights, pl.ANY))
        block_shape = (weights.shape[0], BLOCK) if kind == "up" else (BLOCK, weights.shape[1])
        outs.append(((1, *block_shape), BF16))
        scratch.append(pltpu.SemaphoreType.DMA(()))

    def body(in_refs, out_refs, scratch_refs):
        end = in_refs[0][0] > 0

        def up_copy(i):
            i0, _, s0 = where["up"]
            columns = pl.ds(pl.multiple_of(column_up + i * BLOCK, BLOCK), BLOCK)
            return pltpu.make_async_copy(
                in_refs[i0].at[:, columns], scratch_refs[s0].at[i - kept], scratch_refs[s0 + 1].at[i - kept]
            )

        def down_copy(i):
            i0, _, s0 = where["down"]
            return pltpu.make_async_copy(
                in_refs[i0 + 2].at[pl.ds(column + i * BLOCK, BLOCK), :],
                scratch_refs[s0].at[i - kept],
                scratch_refs[s0 + 1].at[i - kept],
            )

        for i in range(kept, min(kept + IN_FLIGHT, blocks_up)):
            up_copy(i).start()
        for i in range(kept, min(kept + IN_FLIGHT, blocks_down)):
            down_copy(i).start()
        if ahead:
            i4, o4, s4 = where["ahead"]
            span = pl.ds(begin_ahead, BLOCK)
            source = in_refs[i4].at[:, span] if kind == "up" else in_refs[i4].at[span, :]
            ahead_copy = pltpu.make_async_copy(source, out_refs[o4].at[0], scratch_refs[s4])
            ahead_copy.start()

        if add:
            i0, o0 = where["add"]

            def sum_rows(r):
                out_refs[o0][r, :] = (in_refs[i0][r, :].astype(F32) + in_refs[i0 + 1][r, :].astype(F32)).astype(BF16)

            by_rows(add[0].shape[0], 16, sum_rows)
        if act:
            i1, o1 = where["act"]

            @pl.when(jnp.logical_not(end))
            def _():
                def activate(r):
                    v = in_refs[i1][r, :].astype(F32) + in_refs[i1 + 1][r, :].astype(F32)
                    out_refs[o1][r, :] = gelu(v).astype(BF16)

                by_rows(act[0].shape[0], 16, activate)

        if up:
            i2, o2, s2 = where["up"]

            def multiply(i, weights):
                across = shape_up[1] // BLOCK
                columns = pl.ds(pl.multiple_of(i % across * BLOCK, BLOCK), BLOCK)
                begin = pl.multiple_of(i // across * rows_up, rows_up)
                at = 0
                for k, x in enumerate(xs):
                    span = pl.ds(begin + at, x.shape[0])
                    out_refs[o2][span, columns] = jnp.dot(
                        in_refs[i2 + 1 + k][...], weights, preferred_element_type=F32
                    ).astype(BF16)
                    at += x.shape[0]

                if merged:

                    @pl.when(end)
                    def _():
                        span = pl.ds(begin, rows_up)
                        out_refs[where["act"][1]][span, columns] = out_refs[o2][span, columns]

            if kept:

                @pl.loop(0, kept)
                def _(i):
                    multiply(i, in_refs[where["held"][0]][i])

            @pl.loop(kept, blocks_up)
            def _(i):
                up_copy(i).wait()

                @pl.when(i + IN_FLIGHT < blocks_up)
                def _():
                    up_copy(i + IN_FLIGHT).start()

                multiply(i, scratch_refs[s2][i - kept])

        if down:
            i3, o3, s3 = where["down"]
            for i in range(blocks_down):
                if i >= kept:
                    down_copy(i).wait()
                    if i + IN_FLIGHT < blocks_down:
                        down_copy(i + IN_FLIGHT).start()
                across = mine.shape[1] // BLOCK
                units = slice(i % across * BLOCK, (i % across + 1) * BLOCK)
                span = slice(i // across * rows, (i // across + 1) * rows)
                h = jnp.where(end, in_refs[i3 + 1][span, units], in_refs[i3][span, units])
                weights = scratch_refs[s3][i - kept] if i >= kept else in_refs[where["held"][0]][i]
                term = jnp.dot(h, weights, preferred_element_type=F32)
                if first and i == 0:
                    out_refs[o3][row : row + rows, :] = term
                else:
                    out_refs[o3][row : row + rows, :] += term

        if ahead:
            ahead_copy.wait()

    got, passed = chain.call(body, ins, outs, scratch, alias, name, gates, cost)
    return {key: got[at[1]] for key, at in where.items() if at[1] is not None}, passed, merged


def split_rows(chain, features, cut, w_up):
    f, rows = features.shape

    def body(in_refs, out_refs, sems):
        pairs = [
            (in_refs[0].at[:, pl.ds(0, cut)], out_refs[0]),
            (in_refs[0].at[:, pl.ds(cut, rows - cut)], out_refs[1]),
            (in_refs[1].at[:, pl.ds(0, BLOCK)], out_refs[2].at[0]),
        ]
        copies = [pltpu.make_async_copy(a, b, sems[0].at[i]) for i, (a, b) in enumerate(pairs)]
        for copy in copies:
            copy.start()
        for copy in copies:
            copy.wait()

    outs = [((f, cut), BF16), ((f, rows - cut), BF16), ((1, w_up.shape[0], BLOCK), BF16)]
    got, _ = chain.call(
        body, [(features, pltpu.HBM), (w_up, pl.ANY)], outs, [pltpu.SemaphoreType.DMA((3,))], name="split_rows"
    )
    return got


def place_features(chain, place, pieces, name, gates=()):
    f, rows = pieces[0].shape

    def body(in_refs, out_refs, scratch):
        held = scratch[0]
        for mine in range(4):

            @pl.when(in_refs[4][0] == mine)
            def _(mine=mine):
                for q in range(4):
                    held[q * f : (q + 1) * f, :] = in_refs[mine ^ q][...]

        for c in range(0, rows, 128):
            out_refs[0][c : c + 128, :] = held[:, c : c + 128].T

    ins = [(p, pltpu.VMEM) for p in pieces] + [(place, pltpu.SMEM)]
    (x,), passed = chain.call(
        body, ins, [((rows, 4 * f), BF16)], [pltpu.VMEM((4 * f, rows), BF16)], None, name, gates
    )
    return x, passed


def part_features(chain, place, total, row, rows, name, gates=()):
    features = total.shape[1]
    f = features // 4

    def body(in_refs, out_refs, scratch):
        held = scratch[0]
        for c in range(rows // 128):
            held[:, c * 128 : (c + 1) * 128] = (
                in_refs[0][row + c * 128 : row + (c + 1) * 128, :].astype(BF16).T
            )
        for mine in range(4):

            @pl.when(in_refs[1][0] == mine)
            def _(mine=mine):
                for out, slot, q in ((0, 0, mine), (0, 1, mine ^ 2), (1, 0, mine ^ 1), (1, 1, mine ^ 3)):
                    out_refs[out][slot] = held[q * f : (q + 1) * f, :]

    both = ((2, f, rows), BF16)
    (keep, give), passed = chain.call(
        body, [(total, pltpu.VMEM), (place, pltpu.SMEM)], [both, both], [pltpu.VMEM((features, rows), BF16)], None, name, gates
    )
    return keep, give


def add_chip(chain, keep, got, name):
    shape = keep.shape[1:]

    def body(in_refs, out_refs, _):
        for slot in range(2):

            def sum_rows(r, slot=slot):
                out_refs[slot][r, :] = (
                    in_refs[0][slot, r, :].astype(F32) + in_refs[1][slot, r, :].astype(F32)
                ).astype(out_refs[slot].dtype)

            by_rows(shape[0], 16, sum_rows)

    (near, far), _ = chain.call(
        body, [(keep, pltpu.VMEM), (got, pltpu.VMEM)], [(shape, F32), (shape, BF16)], name=name
    )
    return near, far


def finish(chain, near, across, out, shape, row, name, cost=SHORT):
    f, rows = near.shape
    ins, alias = [(near, pltpu.VMEM), (across, pltpu.VMEM)], {}
    if out is not None:
        alias[len(ins)] = 0
        ins.append((out, pltpu.VMEM))

    def body(in_refs, out_refs, _):
        def sum_rows(r):
            out_refs[0][r, row : row + rows] = (in_refs[0][r, :] + in_refs[1][r, :].astype(F32)).astype(BF16)

        by_rows(f, 16, sum_rows)

    (got,), _ = chain.call(body, ins, [(shape, BF16)], alias=alias, name=name, cost=cost)
    return got


def pipelined(tokens, w_up, w_down):
    rows = tokens.shape[0]
    features = tokens.T
    half = rows // 2
    at = lax.axis_index("wide")
    at_end = ((at == 0) | (at == 3)).astype(jnp.int32).reshape(1)
    place = (lax.axis_index("narrow") * 2 + lax.axis_index("sub")).astype(jnp.int32).reshape(1)
    inward, middle, outward = [(0, 1), (3, 2)], [(1, 2), (2, 1)], [(1, 0), (2, 3)]

    chain = Chain(jnp.zeros((8, 128), F32))
    sum_shape = (rows, w_down.shape[1])
    tiles = plan(rows, w_up.shape[1])
    n = len(tiles)

    low, high, held = split_rows(chain, features, half, w_up)
    across = lax.ppermute(low, "narrow", SWAP)
    sibling, corner = lax.ppermute(low, "sub", SWAP), lax.ppermute(across, "sub", SWAP)
    x_low, (high,) = place_features(chain, place, [low, sibling, across, corner], "place_low", gates=(high,))
    xs = {0: x_low}
    across = lax.ppermute(high, "narrow", SWAP)
    sibling = lax.ppermute(high, "sub", SWAP)

    part, summed, hidden = {}, {}, {}
    met_in, met_mid, met_out = {}, {}, {}
    total, seen = None, []
    high_last = max(i for i, tile in enumerate(tiles) if tile[0] + tile[1] > half)
    cost = estimate(STEP_COST)
    reads = []
    for t in range(n + LAG + 1):
        reads += [("up", w_up, tiles[t][2])] if t < n else []
        reads += [("down", w_down, tiles[t - LAG - 1][2])] if 0 <= t - LAG - 1 < n else []
    reads = [*reads[1:], None]
    for t in range(n + LAG + 1):
        g = t - LAG
        up = act = None
        gates = ()
        if t < n:
            if t == 1:
                gates = (across, sibling)
            if half not in xs and tiles[t][0] + tiles[t][1] > half:
                xs[half], _ = place_features(chain, place, [high, sibling, across, corner], "place_high")
            up = ([xs[r] for r in (0, half) if tiles[t][0] <= r < tiles[t][0] + tiles[t][1]], w_up, tiles[t])
        if 0 <= g < n:
            act = (summed[g], met_mid[g])
        if up or act:
            extra = {"held": held, "ahead": reads.pop(0)} if up else {}
            got, passed, merged = step_kernel(
                chain, at_end, f"up_act_{t}", cost, rows, up=up, act=act, gates=gates, **extra
            )
            held = got.get("ahead", held)
            if passed:
                across, sibling = passed
                corner = lax.ppermute(across, "sub", SWAP)
            if up:
                part[t] = got["up"]
            if act:
                hidden[g] = got["act"]
            if merged:
                met_in[t] = met_out[g] = lax.ppermute(got["act"], "wide", inward + outward)
            else:
                if up:
                    met_in[t] = lax.ppermute(got["up"], "wide", inward)
                if act:
                    met_out[g] = lax.ppermute(got["act"], "wide", outward)
        a, d = t - 1, t - LAG - 1
        add = down = None
        if 0 <= a < n:
            add = (part[a], met_in[a])
        if 0 <= d < n:
            first = not any(r < tiles[d][0] + tiles[d][1] and tiles[d][0] < r + k for r, k in seen)
            seen.append(tiles[d][:2])
            down = (hidden[d], met_out[d], w_down, tiles[d], total, sum_shape, first)
        if add or down:
            extra = {"held": held, "ahead": reads.pop(0)} if down else {}
            got, _, _ = step_kernel(chain, at_end, f"add_down_{t}", cost, rows, add=add, down=down, **extra)
            held = got.get("ahead", held)
            if add:
                summed[a] = got["add"]
                met_mid[a] = lax.ppermute(got["add"], "wide", middle)
            if down:
                total = got["down"]
        if d == high_last:
            keep, give = part_features(chain, place, total, half, rows - half, "part_high")
            got_high = lax.ppermute(give, "sub", SWAP)
        if d == high_last + 1:
            near, chip = add_chip(chain, keep, got_high, "add_chip_high")
            high_sum = (near, lax.ppermute(chip, "narrow", SWAP))

    keep, give = part_features(chain, place, total, 0, half, "part_low")
    out = finish(chain, *high_sum, None, features.shape, half, "finish_high", cost)
    near, chip = add_chip(chain, keep, lax.ppermute(give, "sub", SWAP), "add_chip_low")
    across = lax.ppermute(chip, "narrow", SWAP)
    return finish(chain, near, across, out, features.shape, 0, "finish_low").T


def collective(tokens, w_up, w_down):
    gathered = lax.all_gather(tokens, ("narrow", "sub"), axis=1, tiled=True)
    block_up = jnp.dot(gathered, w_up, preferred_element_type=F32).astype(BF16)
    pre = lax.psum_scatter(block_up, "wide", scatter_dimension=1, tiled=True).astype(F32)
    hidden = lax.all_gather(gelu(pre).astype(BF16), "wide", axis=1, tiled=True)
    block_down = jnp.dot(hidden, w_down, preferred_element_type=F32).astype(BF16)
    return lax.psum_scatter(block_down, ("narrow", "sub"), scatter_dimension=1, tiled=True)


def solution(mesh):
    placed = (
        P("groups", ("wide", "narrow", "sub")),
        P("wide", ("narrow", "sub")),
        P(("narrow", "sub"), "wide"),
    )
    small = (mesh.shape["wide"], mesh.shape["narrow"], mesh.shape["sub"]) == (4, 2, 2)
    return jax.shard_map(
        pipelined if small else collective,
        mesh=mesh,
        in_specs=placed,
        out_specs=P("groups", ("wide", "narrow", "sub")),
        check_vma=False,
    )
```
